32 devices in a mesh: dom: 16 (over z, y, x), col: 2 (over core).
Axes of the slice: x: 2, y: 2, z: 4, core: 2. Of those that a mesh axis runs over, the one named last changes fastest.
Arguments:
- src_local: int32 [32768], P('dom'), may hold values from 0 to 4095
- dst_local: int32 [32768], P('dom'), may hold values from 0 to 4095
- edge_weight: float32 [32768], P('dom'), may hold values from 0.25 to 4
- send_counts: int32 [16, 16], P('dom'), may hold values from 1 to 128, as said below
- sketch: bfloat16 [128, 32768], P('col', 'dom'), may hold values from -6 to 6
Outputs:
- solution: float32 [128, 65536], P('col', 'dom')
- resistance: float32 [32768], P('dom')
The draws below stay inside these ranges and needn't reach their ends.
Inputs may be any that keep to these rules, and one draw needn't show every extreme that they name: Each row of send_counts reaches 128 for some peer, and one peer receives 128 live slots from every partition.
All inputs are finite; a program needn't handle non-finite values.
Results may differ from the reference program's by a relative error of at most 0.0003.
Values sent between devices are 32-bit elements; how exact they have to be, the bound alone decides.
A program may use at most 64 MiB of HBM per device.

```python
import math
import jax
import jax.numpy as jnp
import numpy as np
from jax import lax

SKETCH = 128
VERT_DEV = 4096
EDGE_DEV = 2048
SWEEPS = 3
EDGES = 32768
N_DOM = 16


def draw_send_counts(key, part):
    cap = EDGE_DEV // N_DOM
    levels = cap.bit_length()
    level_key = jax.random.fold_in(key, 11)
    pick_key = jax.random.fold_in(key, 12)
    busy_key = jax.random.fold_in(key, 13)
    coin_key = jax.random.fold_in(key, 14)
    level = jax.random.randint(level_key, (N_DOM, N_DOM), 0, levels)
    coin = jax.random.randint(coin_key, (N_DOM, N_DOM), 0, 2)
    level = level * coin
    counts = jnp.maximum(jnp.right_shift(jnp.full((N_DOM, N_DOM), cap, jnp.int32), level), 1)
    picked = jax.random.randint(pick_key, (N_DOM,), 0, N_DOM)
    busiest = jax.random.randint(busy_key, (), 0, N_DOM)
    columns = jnp.arange(N_DOM)[None, :]
    full = (columns == picked[:, None]) | (columns == busiest)
    return jnp.where(full, cap, counts).astype(jnp.int32)


def set_ends(entries, key, least, high):
    spot = [jax.random.randint(jax.random.fold_in(key, axis), (), 0, length) for axis, length in enumerate(entries.shape)]
    longest = entries.shape.index(max(entries.shape))
    next_to = spot[:longest] + [(spot[longest] + 1) % entries.shape[longest]] + spot[longest + 1:]
    return entries.at[tuple(spot)].set(least).at[tuple(next_to)].set(high)


def block_scale(rng, shape, pieces, low, top_value):
    loudness = 1.0
    for position, shards_of in pieces:
        heights = jax.random.uniform(jax.random.fold_in(jax.random.fold_in(rng, 6), position), (shards_of,), jnp.float32, low / len(pieces), top_value / len(pieces))
        loudness = loudness * jnp.repeat(jnp.exp(heights), shape[position] // shards_of).reshape((-1,) + (1,) * (len(shape) - 1 - position))
    return loudness


def rank_bounds(number_of, slope):
    loads = [(1 << 20) // math.isqrt(standing ** slope) + 1 for standing in range(1, number_of + 1)]
    width = 1 + sum(loads) // (1 << 30)
    return np.cumsum(np.array([max(1, weight // width) for weight in loads]))


def ranked(rng, shape, number_of, lean):
    grid = rank_bounds(number_of, lean)
    pick = jax.random.randint(jax.random.fold_in(rng, 1), shape, 0, int(grid[number_of - 1]))
    rank = jnp.searchsorted(jnp.asarray(grid, jnp.int32), pick, side="right")
    return jax.random.permutation(jax.random.fold_in(rng, 2), number_of)[rank].astype(jnp.int32)


def noise(key, dims, spread, most, split=(), kind=jnp.bfloat16):
    factor_of = block_scale(key, dims, split, -0.22, 0.18) if split else 1.0
    result = jax.random.normal(key, dims, jnp.float32) * spread * factor_of
    return jnp.minimum(jnp.maximum(result, -most), most).astype(kind)


def setup_inputs(seed: int = 0) -> dict:
    arg_keys = jax.random.split(jax.random.key(seed), 6)
    return {
        "src_local": set_ends(ranked(arg_keys[0], (EDGES,), VERT_DEV, 2), jax.random.fold_in(arg_keys[0], 3), 0, VERT_DEV - 1).astype(jnp.int32),
        "dst_local": set_ends(ranked(arg_keys[1], (EDGES,), VERT_DEV, 2), jax.random.fold_in(arg_keys[1], 3), 0, VERT_DEV - 1).astype(jnp.int32),
        "edge_weight": jnp.clip(jnp.exp(math.log(4.0) - 2.7725887 * jax.random.uniform(arg_keys[2], (EDGES,), jnp.float32) ** block_scale(arg_keys[2], (EDGES,), ((0, 16),), -0.2, 0.2)), 0.25, 4.0),
        "send_counts": draw_send_counts(jax.random.fold_in(arg_keys[5], 71), 0),
        "sketch": noise(arg_keys[4], (SKETCH, EDGES), 1.0, 6.0, ((0, 2), (1, 16))),
    }


ground_shift = 1.0
degree_boost = 0.25

def reference(src_local, dst_local, edge_weight, send_counts, sketch):
    cap = EDGE_DEV // N_DOM
    slot = jnp.arange(N_DOM * EDGE_DEV, dtype=jnp.int32)
    owner = slot // EDGE_DEV
    within = slot % EDGE_DEV
    peer = within // cap
    place = within % cap
    live = (place < send_counts[owner, peer]).astype(jnp.float32)
    first = owner * VERT_DEV + src_local
    second = peer * VERT_DEV + dst_local
    weights = edge_weight * live
    count = N_DOM * VERT_DEV
    root = jnp.sqrt(weights)[None, :] * sketch.astype(jnp.float32)
    zero_rows = jnp.zeros((SKETCH, count), jnp.float32)
    rhs = zero_rows.at[:, first].add(root).at[:, second].add(-root)
    degree = jnp.zeros((count,), jnp.float32).at[first].add(weights).at[second].add(weights)
    diag = (1.0 + degree_boost) * degree + ground_shift
    extra = degree_boost * degree + ground_shift

    def apply(field):
        flow = weights[None, :] * (field[:, first] - field[:, second])
        return zero_rows.at[:, first].add(flow).at[:, second].add(-flow) + extra[None, :] * field
    sigma = 1.25
    delta = 0.8
    coeff = 1.0 / sigma
    resid = rhs
    direction = resid / diag[None, :]
    solution = zero_rows
    for sweep in range(SWEEPS):
        solution = solution + direction
        if sweep < SWEEPS - 1:
            resid = resid - apply(direction)
            newer = 1.0 / (2.0 * sigma - coeff)
            direction = newer * coeff * direction + 2.0 * newer / delta * resid / diag[None, :]
            coeff = newer
    diff = solution[:, first] - solution[:, second]
    resistance = lax.optimization_barrier(jnp.sum(diff * diff, axis=0)) / SKETCH * live
    return (solution, resistance)
```

```python
import functools

import jax
import jax.numpy as jnp
from jax import lax
from jax.experimental import pallas as pl
from jax.experimental.pallas import tpu as pltpu
from jax.sharding import PartitionSpec as P

MESH = pl.DeviceIdType.MESH
F32 = jnp.float32
BF16 = jnp.bfloat16
VERT_DEV = 4096
SKETCH = 128
SWEEPS = 3
LANES = 128
HALF = 64
ground_shift = 1.0
degree_boost = 0.25


def either(a, b, n):
    total, bit = 0, 1
    while bit < n:
        total = total + bit * lax.rem(lax.div(a, bit) + lax.div(b, bit), 2)
        bit *= 2
    return total


def kernel(
    peers, cap, meta_ref, root_ref, src_ref, weight_ref, live_ref, sol_ref, res_ref,
    same, ids, rows, acc, field, resid, total, inv, keep, wide, ends, part, part_in,
    meta_in, root_in, one_in, two_in, last_out, last_in,
    meta_s, meta_r, even_s, even_r, odd_s, odd_r, part_s, part_r,
):
    me = lax.axis_index("dom")
    other = 1 - lax.axis_index("col")
    group = LANES // cap
    count = peers // group
    own_group = lax.div(me, group)

    barrier = pltpu.get_barrier_semaphore()

    def greet(i, _):
        pl.semaphore_signal(barrier, inc=1, device_id={"dom": either(me, i, peers)}, device_id_type=MESH)
        return 0

    lax.fori_loop(1, peers, greet, 0)
    pl.semaphore_signal(barrier, inc=1, device_id={"col": other}, device_id_type=MESH)
    pl.semaphore_wait(barrier, peers)

    def copy(p, source, target, s, r):
        return pltpu.make_async_remote_copy(
            src_ref=source.at[p], dst_ref=target.at[me], send_sem=s.at[p], recv_sem=r.at[me],
            device_id={"dom": p}, device_id_type=MESH,
        )

    def arrival(p, source, target, s, r):
        return pltpu.make_async_remote_copy(
            src_ref=source.at[p], dst_ref=target.at[p], send_sem=s.at[p], recv_sem=r.at[p],
            device_id={"dom": p}, device_id_type=MESH,
        )

    def send_group(far, source, target, s, r):
        for j in range(group):
            i = far * group + j
            p = either(me, i, peers)

            @pl.when(i != 0)
            def _():
                copy(p, source, target, s, r).start()

            @pl.when(i == 0)
            def _():
                target[me] = source[me]

    def wait_group(far, source, target, s, r):
        for j in range(group):
            i = far * group + j
            p = either(me, i, peers)

            @pl.when(i != 0)
            def _():
                arrival(p, source, target, s, r).wait_recv()

    def wait_sent(source, target, s, r):
        def step(i, _):
            copy(either(me, i, peers), source, target, s, r).wait_send()
            return 0

        lax.fori_loop(1, peers, step, 0)

    low = lax.broadcasted_iota(jnp.int32, (LANES, LANES), 1) < HALF

    def mask(a):
        return low[: a.shape[0]]

    def turned(a):
        return pltpu.roll(a, HALF, axis=1)

    def doubled(a):
        b = turned(a)
        return jnp.where(mask(a), a, b), jnp.where(mask(a), b, a)

    def split(a):
        high = a.astype(BF16).astype(F32)
        return jnp.where(low, high, a - high).astype(BF16)

    def column(row):
        return jnp.broadcast_to(row, (LANES, LANES)).T

    def unfold(ref, g):
        pieces = []
        for j in range(group):
            pieces.extend(doubled(ref[g * group + j]))
        return jnp.concatenate(pieces, axis=0)

    def block(ref, g):
        return ref[pl.ds(g * group, group)].reshape(LANES, LANES)

    def near_first(t):
        return either(own_group, lax.rem(count - t, count), count), lax.rem(count - t, count)

    def send_meta(t, _):
        send_group(count - 1 - t, meta_ref, meta_in, meta_s, meta_r)
        return 0

    lax.fori_loop(0, count, send_meta, 0)

    def send_root(t, _):
        send_group(count - 1 - t, root_ref, root_in, even_s, even_r)
        return 0

    lax.fori_loop(0, count, send_root, 0)

    def first_ends(g, _):
        row = src_ref[pl.ds(g, 1), :]
        rows[g, 0:1] = row
        ids[g] = column(row)
        wide[g] = column(weight_ref[pl.ds(g, 1), :])
        return 0

    lax.fori_loop(0, count, first_ends, 0)

    def second_ends(t, _):
        g, far = near_first(t)
        wait_group(far, meta_ref, meta_in, meta_s, meta_r)
        named = [column(meta_in[g * group + j][0:1])[:cap] for j in range(group)]
        named = jnp.concatenate(named, axis=0)
        heavy = [column(meta_in[g * group + j][1:2])[:cap] for j in range(group)]
        heavy = jnp.concatenate(heavy, axis=0)
        ids[count + g] = named
        rows[g, 1:2] = named.T[0:1]
        wide[count + g] = heavy
        return 0

    lax.fori_loop(0, count, second_ends, 0)

    tile = 512
    blocks = tile // LANES
    tiles = 2 * count // blocks

    acc[...] = jnp.zeros_like(acc)

    def first_product(t, _):
        g, far = near_first(t)
        wait_group(far, root_ref, root_in, even_s, even_r)
        value = jnp.concatenate([split(unfold(root_ref, g)), split(-unfold(root_in, g))], axis=0)
        load = jnp.concatenate([split(wide[g]), split(wide[count + g])], axis=0)
        x = jnp.concatenate([value, load], axis=1)
        row_u, row_v = rows[g, 0:1], rows[g, 1:2]

        def step(k, _):
            at = pl.ds(pl.multiple_of(k * tile, tile), tile)
            name = ids[pl.ds(k * blocks, blocks)].reshape(tile, LANES)
            e = jnp.concatenate(
                [jnp.where(name == row_u, 1.0, 0.0), jnp.where(name == row_v, 1.0, 0.0)], axis=1
            ).astype(BF16)
            same[g, at, :] = e
            acc[at, :] += jnp.dot(e, x, preferred_element_type=F32)
            return 0

        lax.fori_loop(0, tiles, step, 0)
        return 0

    lax.fori_loop(0, count, first_product, 0)
    wait_sent(meta_ref, meta_in, meta_s, meta_r)
    wait_sent(root_ref, root_in, even_s, even_r)

    def at_ends(g, lane):
        a = acc[pl.ds(pl.multiple_of(g * LANES, LANES), LANES), lane : lane + LANES]
        b = acc[pl.ds(pl.multiple_of((count + g) * LANES, LANES), LANES), lane : lane + LANES]
        return jnp.where(low, a + turned(a), b + turned(b))

    def put(ref, g, value):
        ref[pl.ds(g * group, group)] = value.reshape(group, cap, LANES)

    def start_field(t, _):
        far = count - 1 - t
        g = either(own_group, far, count)
        degree = at_ends(g, LANES)
        one_over = 1.0 / ((1.0 + degree_boost) * degree + ground_shift)
        inv[g] = one_over
        keep[g] = (degree_boost * degree + ground_shift) * one_over
        d = at_ends(g, 0) * one_over
        put(field, g, d)
        send_group(far, field, one_in, odd_s, odd_r)
        resid[g] = d
        total[g] = d
        wide[g] = jnp.where(low, wide[g], wide[count + g])
        return 0

    lax.fori_loop(0, count, start_field, 0)

    def multiply(came, s, r):
        acc[:, 0:LANES] = jnp.zeros((2 * count * LANES, LANES), F32)

        def product(t, _):
            g, far = near_first(t)
            wait_group(far, field, came, s, r)
            flow = wide[g] * (block(field, g) - turned(block(came, g)))
            flow_u, flow_v = doubled(flow)
            x = jnp.concatenate([split(flow_u), split(flow_v)], axis=0)

            def step(k, _):
                at = pl.ds(pl.multiple_of(k * tile, tile), tile)
                acc[at, 0:LANES] += jnp.dot(same[g, at, :], x, preferred_element_type=F32)
                return 0

            lax.fori_loop(0, tiles, step, 0)
            return 0

        lax.fori_loop(0, count, product, 0)
        wait_sent(field, came, s, r)

    sigma, delta = 1.25, 0.8
    coeff = 1.0 / sigma
    newer = 1.0 / (2.0 * sigma - coeff)
    pairs = ((newer * coeff, 2.0 * newer / delta),)
    coeff = newer
    newer = 1.0 / (2.0 * sigma - coeff)
    pairs += ((newer * coeff, 2.0 * newer / delta),)

    multiply(one_in, odd_s, odd_r)

    def second_field(t, _):
        far = count - 1 - t
        g = either(own_group, far, count)
        d = block(field, g)
        r = resid[g] - (at_ends(g, 0) * inv[g] + keep[g] * d)
        d = pairs[0][0] * d + pairs[0][1] * r
        put(field, g, d)
        send_group(far, field, two_in, even_s, even_r)
        resid[g] = r
        total[g] = total[g] + d
        return 0

    lax.fori_loop(0, count, second_field, 0)
    multiply(two_in, even_s, even_r)

    def third_field(t, _):
        far = count - 1 - t
        g = either(own_group, far, count)
        d = block(field, g)
        r = resid[g] - (at_ends(g, 0) * inv[g] + keep[g] * d)
        d = pairs[1][0] * d + pairs[1][1] * r
        whole = total[g] + d
        total[g] = whole
        for j in range(group):
            a = whole[j * cap : j * cap + cap // 2]
            b = whole[j * cap + cap // 2 : (j + 1) * cap]
            last_out[g * group + j] = jnp.where(mask(a), turned(a), b)
        send_group(far, last_out, last_in, odd_s, odd_r)
        whole_u, whole_v = doubled(whole)
        ones = jnp.ones((LANES, LANES), BF16)
        ends[g, 0:LANES, :] = jnp.concatenate([split(whole_u), ones], axis=1)
        ends[g, LANES:, :] = jnp.concatenate([split(whole_v), ones], axis=1)
        return 0

    lax.fori_loop(0, count, third_field, 0)

    strip = 256

    def vertices(k, _):
        first = k * strip
        name = (lax.broadcasted_iota(jnp.int32, (strip, LANES), 0) + first).astype(F32)
        out = jnp.zeros((strip, 2 * LANES), F32)
        for g in range(count):
            e = jnp.concatenate(
                [jnp.where(name == rows[g, 0:1], 1.0, 0.0), jnp.where(name == rows[g, 1:2], 1.0, 0.0)], axis=1
            ).astype(BF16)
            out = out + jnp.dot(e, ends[g], preferred_element_type=F32)
        value = out[:, 0:LANES]
        value = (value + turned(value)) / jnp.maximum(out[:, LANES:], 1.0)
        sol_ref[:, pl.ds(pl.multiple_of(first, strip), strip)] = value.T[0:HALF]
        return 0

    lax.fori_loop(0, VERT_DEV // strip, vertices, 0)

    def differences(t, _):
        g, far = near_first(t)
        wait_group(far, last_out, last_in, odd_s, odd_r)
        diff = jnp.where(low, total[g] - unfold(last_in, g), 0.0)
        part[pl.ds(g, 1), :] = jnp.sum((diff * diff).T, axis=0, keepdims=True)
        return 0

    lax.fori_loop(0, count, differences, 0)
    wait_sent(last_out, last_in, odd_s, odd_r)

    swap = pltpu.make_async_remote_copy(
        src_ref=part, dst_ref=part_in, send_sem=part_s, recv_sem=part_r,
        device_id={"col": other}, device_id_type=MESH,
    )
    swap.start()
    swap.wait()
    res_ref[...] = (part[...] + part_in[...]) / SKETCH * live_ref[...]


def local(src_local, dst_local, edge_weight, send_counts, sketch):
    peers = lax.axis_size("dom")
    edges = src_local.shape[0]
    cap = edges // peers
    width = sketch.shape[0]
    count = edges // LANES
    live = (jnp.arange(cap)[None, :] < send_counts.reshape(peers, 1)).astype(F32)
    weight = edge_weight.reshape(peers, cap) * live
    root = (jnp.sqrt(weight).reshape(1, edges) * sketch.astype(F32)).reshape(width, peers, 2, cap // 2)
    root = root.transpose(1, 3, 2, 0).reshape(peers, cap // 2, LANES)
    meta = jnp.stack([dst_local.reshape(peers, cap).astype(F32), weight], axis=1)
    meta = jnp.pad(meta, ((0, 0), (0, 6), (0, LANES - cap)))
    vmem = functools.partial(pl.BlockSpec, memory_space=pltpu.VMEM)
    dma = pltpu.SemaphoreType.DMA
    wide = pltpu.VMEM((count, LANES, LANES), F32)
    whole = pltpu.VMEM((peers, cap, LANES), F32)
    half = pltpu.VMEM((peers, cap // 2, LANES), F32)
    solution, resistance = pl.pallas_call(
        functools.partial(kernel, peers, cap),
        out_shape=(jax.ShapeDtypeStruct((width, VERT_DEV), F32), jax.ShapeDtypeStruct((count, LANES), F32)),
        in_specs=[vmem()] * 5,
        out_specs=(vmem(), vmem()),
        scratch_shapes=[
            pltpu.VMEM((count, 2 * edges, 2 * LANES), BF16),
            pltpu.VMEM((2 * count, LANES, LANES), F32),
            pltpu.VMEM((count, 8, LANES), F32),
            pltpu.VMEM((2 * edges, 2 * LANES), F32),
            whole, wide, wide, wide, wide,
            pltpu.VMEM((2 * count, LANES, LANES), F32),
            pltpu.VMEM((count, 2 * LANES, 2 * LANES), BF16),
            pltpu.VMEM((count, LANES), F32),
            pltpu.VMEM((count, LANES), F32),
            pltpu.VMEM((peers, 8, LANES), F32),
            half, whole, whole, half, half,
            dma((peers,)), dma((peers,)), dma((peers,)), dma((peers,)), dma((peers,)), dma((peers,)),
            dma, dma,
        ],
        compiler_params=pltpu.CompilerParams(
            collective_id=0, has_side_effects=True, vmem_limit_bytes=60 * 1024 * 1024
        ),
    )(meta, root, src_local.astype(F32).reshape(count, LANES), weight.reshape(count, LANES), live.reshape(count, LANES))
    return solution, resistance.reshape(edges)


def solution(mesh):
    in_specs = (P("dom"), P("dom"), P("dom"), P("dom", None), P("col", "dom"))
    out_specs = (P("col", "dom"), P("dom"))
    return jax.shard_map(local, mesh=mesh, in_specs=in_specs, out_specs=out_specs, check_vma=False)
```

```python
import functools

import jax
import jax.numpy as jnp
from jax import lax
from jax.experimental import pallas as pl
from jax.experimental.pallas import tpu as pltpu
from jax.sharding import PartitionSpec as P

MESH = pl.DeviceIdType.MESH
F32 = jnp.float32
BF16 = jnp.bfloat16
VERT_DEV = 4096
SKETCH = 128
SWEEPS = 3
LANES = 128
HALF = 64
ground_shift = 1.0
degree_boost = 0.25


def either(a, b, n):
    total, bit = 0, 1
    while bit < n:
        total = total + bit * lax.rem(lax.div(a, bit) + lax.div(b, bit), 2)
        bit *= 2
    return total


def kernel(
    peers, cap, counts_ref, src_ref, dst_ref, flat_ref, weight_ref, sketch_ref, sol_ref, res_ref,
    same, ids, rows, acc, field, resid, total, inv, keep, wide, ends, part, part_in,
    live_ref, meta_ref, root_ref, meta_in, root_in, one_in, two_in, last_out, last_in,
    meta_s, meta_r, even_s, even_r, odd_s, odd_r, part_s, part_r,
):
    me = lax.axis_index("dom")
    other = 1 - lax.axis_index("col")
    group = LANES // cap
    count = peers // group
    own_group = lax.div(me, group)

    barrier = pltpu.get_barrier_semaphore()

    def greet(i, _):
        pl.semaphore_signal(barrier, inc=1, device_id={"dom": either(me, i, peers)}, device_id_type=MESH)
        return 0

    lax.fori_loop(1, peers, greet, 0)
    pl.semaphore_signal(barrier, inc=1, device_id={"col": other}, device_id_type=MESH)

    def copy(p, source, target, s, r):
        return pltpu.make_async_remote_copy(
            src_ref=source.at[p], dst_ref=target.at[me], send_sem=s.at[p], recv_sem=r.at[me],
            device_id={"dom": p}, device_id_type=MESH,
        )

    def arrival(p, source, target, s, r):
        return pltpu.make_async_remote_copy(
            src_ref=source.at[p], dst_ref=target.at[p], send_sem=s.at[p], recv_sem=r.at[p],
            device_id={"dom": p}, device_id_type=MESH,
        )

    def send_group(far, source, target, s, r):
        for j in range(group):
            i = far * group + j
            p = either(me, i, peers)

            @pl.when(i != 0)
            def _():
                copy(p, source, target, s, r).start()

            @pl.when(i == 0)
            def _():
                target[me] = source[me]

    def wait_group(far, source, target, s, r):
        for j in range(group):
            i = far * group + j
            p = either(me, i, peers)

            @pl.when(i != 0)
            def _():
                arrival(p, source, target, s, r).wait_recv()

    def wait_sent(source, target, s, r):
        def step(i, _):
            copy(either(me, i, peers), source, target, s, r).wait_send()
            return 0

        lax.fori_loop(1, peers, step, 0)

    low = lax.broadcasted_iota(jnp.int32, (LANES, LANES), 1) < HALF

    def mask(a):
        return low[: a.shape[0]]

    def turned(a):
        return pltpu.roll(a, HALF, axis=1)

    def doubled(a):
        b = turned(a)
        return jnp.where(mask(a), a, b), jnp.where(mask(a), b, a)

    def split(a):
        high = a.astype(BF16).astype(F32)
        return jnp.where(low, high, a - high).astype(BF16)

    def column(row):
        return jnp.broadcast_to(row, (LANES, LANES)).T

    def unfold(ref, g):
        pieces = []
        for j in range(group):
            pieces.extend(doubled(ref[g * group + j]))
        return jnp.concatenate(pieces, axis=0)

    def block(ref, g):
        return ref[pl.ds(g * group, group)].reshape(LANES, LANES)

    def near_first(t):
        return either(own_group, lax.rem(count - t, count), count), lax.rem(count - t, count)

    spot = lax.broadcasted_iota(jnp.int32, (1, LANES), 1)

    def message(p, _):
        alive = jnp.where(spot[:, :cap] < counts_ref[0, p], 1.0, 0.0)
        meta_ref[p, 0:1, 0:cap] = dst_ref[pl.ds(p, 1), :].astype(F32)
        meta_ref[p, 1:2, 0:cap] = flat_ref[pl.ds(p, 1), :] * alive
        return 0

    meta_ref[...] = jnp.zeros_like(meta_ref)
    lax.fori_loop(0, peers, message, 0, unroll=4)
    pl.semaphore_wait(barrier, peers)

    def send_meta(t, _):
        send_group(count - 1 - t, meta_ref, meta_in, meta_s, meta_r)
        return 0

    lax.fori_loop(0, count, send_meta, 0)

    def send_root(t, _):
        far = count - 1 - t
        g = either(own_group, far, count)
        alive = jnp.zeros((1, LANES), F32)
        for j in range(group):
            there = (spot >= j * cap) & (spot < j * cap + counts_ref[0, g * group + j])
            alive = jnp.where(there, 1.0, alive)
        live_ref[pl.ds(g, 1), :] = alive
        heavy = weight_ref[pl.ds(g, 1), :] * alive
        wide[g] = column(heavy)
        at = pl.ds(pl.multiple_of(g * LANES, LANES), LANES)
        value = jnp.sqrt(heavy) * sketch_ref[:, at].astype(F32)
        value = jnp.concatenate([value, value], axis=0).T
        total[g] = value
        for j in range(group):
            a = value[j * cap : j * cap + cap // 2]
            b = value[j * cap + cap // 2 : (j + 1) * cap]
            root_ref[g * group + j] = jnp.where(mask(a), a, b)
        send_group(far, root_ref, root_in, even_s, even_r)
        return 0

    lax.fori_loop(0, count, send_root, 0)

    def first_ends(g, _):
        row = src_ref[pl.ds(g, 1), :].astype(F32)
        rows[g, 0:1] = row
        ids[g] = column(row)
        return 0

    lax.fori_loop(0, count, first_ends, 0, unroll=4)

    def take_meta(t, _):
        wait_group(t, meta_ref, meta_in, meta_s, meta_r)
        return 0

    lax.fori_loop(0, count, take_meta, 0)

    def second_ends(g, _):
        named = [column(meta_in[g * group + j][0:1])[:cap] for j in range(group)]
        named = jnp.concatenate(named, axis=0)
        heavy = [column(meta_in[g * group + j][1:2])[:cap] for j in range(group)]
        heavy = jnp.concatenate(heavy, axis=0)
        ids[count + g] = named
        rows[g, 1:2] = named.T[0:1]
        wide[count + g] = heavy
        return 0

    lax.fori_loop(0, count, second_ends, 0, unroll=4)

    tile = 512
    blocks = tile // LANES
    tiles = 2 * count // blocks

    acc[...] = jnp.zeros_like(acc)

    def first_product(t, _):
        g, far = near_first(t)
        wait_group(far, root_ref, root_in, even_s, even_r)
        value = jnp.concatenate([split(total[g]), split(-unfold(root_in, g))], axis=0)
        load = jnp.concatenate([split(wide[g]), split(wide[count + g])], axis=0)
        x = jnp.concatenate([value, load], axis=1)
        row_u, row_v = rows[g, 0:1], rows[g, 1:2]

        for k in range(tiles):
            at = pl.ds(k * tile, tile)
            name = ids[pl.ds(k * blocks, blocks)].reshape(tile, LANES)
            e = jnp.concatenate(
                [jnp.where(name == row_u, 1.0, 0.0), jnp.where(name == row_v, 1.0, 0.0)], axis=1
            ).astype(BF16)
            same[g, at, :] = e
            acc[at, :] += jnp.dot(e, x, preferred_element_type=F32)
        return 0

    lax.fori_loop(0, count, first_product, 0)
    wait_sent(meta_ref, meta_in, meta_s, meta_r)
    wait_sent(root_ref, root_in, even_s, even_r)

    def at_ends(g, lane):
        a = acc[pl.ds(pl.multiple_of(g * LANES, LANES), LANES), lane : lane + LANES]
        b = acc[pl.ds(pl.multiple_of((count + g) * LANES, LANES), LANES), lane : lane + LANES]
        return jnp.where(low, a + turned(a), b + turned(b))

    def put(ref, g, value):
        ref[pl.ds(g * group, group)] = value.reshape(group, cap, LANES)

    def start_field(t, _):
        far = count - 1 - t
        g = either(own_group, far, count)
        degree = at_ends(g, LANES)
        one_over = 1.0 / ((1.0 + degree_boost) * degree + ground_shift)
        inv[g] = one_over
        keep[g] = (degree_boost * degree + ground_shift) * one_over
        d = at_ends(g, 0) * one_over
        put(field, g, d)
        send_group(far, field, one_in, odd_s, odd_r)
        resid[g] = d
        total[g] = d
        wide[g] = jnp.where(low, wide[g], wide[count + g])
        return 0

    lax.fori_loop(0, count, start_field, 0)

    def multiply(came, s, r):
        acc[:, 0:LANES] = jnp.zeros((2 * count * LANES, LANES), F32)

        def product(t, _):
            g, far = near_first(t)
            wait_group(far, field, came, s, r)
            flow = wide[g] * (block(field, g) - turned(block(came, g)))
            flow_u, flow_v = doubled(flow)
            x = jnp.concatenate([split(flow_u), split(flow_v)], axis=0)

            for k in range(tiles):
                at = pl.ds(k * tile, tile)
                acc[at, 0:LANES] += jnp.dot(same[g, at, :], x, preferred_element_type=F32)
            return 0

        lax.fori_loop(0, count, product, 0)
        wait_sent(field, came, s, r)

    sigma, delta = 1.25, 0.8
    coeff = 1.0 / sigma
    newer = 1.0 / (2.0 * sigma - coeff)
    pairs = ((newer * coeff, 2.0 * newer / delta),)
    coeff = newer
    newer = 1.0 / (2.0 * sigma - coeff)
    pairs += ((newer * coeff, 2.0 * newer / delta),)

    multiply(one_in, odd_s, odd_r)

    def second_field(t, _):
        far = count - 1 - t
        g = either(own_group, far, count)
        d = block(field, g)
        r = resid[g] - (at_ends(g, 0) * inv[g] + keep[g] * d)
        d = pairs[0][0] * d + pairs[0][1] * r
        put(field, g, d)
        send_group(far, field, two_in, even_s, even_r)
        resid[g] = r
        total[g] = total[g] + d
        return 0

    lax.fori_loop(0, count, second_field, 0)
    multiply(two_in, even_s, even_r)

    def third_field(t, _):
        far = count - 1 - t
        g = either(own_group, far, count)
        d = block(field, g)
        r = resid[g] - (at_ends(g, 0) * inv[g] + keep[g] * d)
        d = pairs[1][0] * d + pairs[1][1] * r
        whole = total[g] + d
        total[g] = whole
        for j in range(group):
            a = whole[j * cap : j * cap + cap // 2]
            b = whole[j * cap + cap // 2 : (j + 1) * cap]
            last_out[g * group + j] = jnp.where(mask(a), turned(a), b)
        send_group(far, last_out, last_in, odd_s, odd_r)
        whole_u, whole_v = doubled(whole)
        ones = jnp.ones((2 * LANES, LANES), BF16)
        pair = jnp.concatenate([split(whole_u), split(whole_v)], axis=0)
        at = pl.ds(pl.multiple_of(g * 2 * LANES, 2 * LANES), 2 * LANES)
        ends[at, :] = jnp.concatenate([pair, ones], axis=1)
        return 0

    lax.fori_loop(0, count, third_field, 0)

    strip = 256

    def vertices(k, _):
        first = k * strip
        name = (lax.broadcasted_iota(jnp.int32, (strip, LANES), 0) + first).astype(F32)
        e = [
            jnp.where(name == rows[g, j : j + 1], 1.0, 0.0).astype(BF16) for g in range(count) for j in range(2)
        ]
        out = jnp.dot(jnp.concatenate(e, axis=1), ends[...], preferred_element_type=F32)
        value = out[:, 0:LANES]
        value = (value + turned(value)) / jnp.maximum(out[:, LANES:], 1.0)
        sol_ref[:, pl.ds(pl.multiple_of(first, strip), strip)] = value.T[0:HALF]
        return 0

    lax.fori_loop(0, VERT_DEV // strip, vertices, 0)

    def differences(t, _):
        g, far = near_first(t)
        wait_group(far, last_out, last_in, odd_s, odd_r)
        diff = jnp.where(low, total[g] - unfold(last_in, g), 0.0)
        part[pl.ds(g, 1), :] = jnp.sum((diff * diff).T, axis=0, keepdims=True)
        return 0

    lax.fori_loop(0, count, differences, 0)
    wait_sent(last_out, last_in, odd_s, odd_r)

    swap = pltpu.make_async_remote_copy(
        src_ref=part, dst_ref=part_in, send_sem=part_s, recv_sem=part_r,
        device_id={"col": other}, device_id_type=MESH,
    )
    swap.start()
    swap.wait()
    res_ref[...] = (part[...] + part_in[...]) / SKETCH * live_ref[...]


def local(src_local, dst_local, edge_weight, send_counts, sketch):
    peers = lax.axis_size("dom")
    edges = src_local.shape[0]
    cap = edges // peers
    width = sketch.shape[0]
    count = edges // LANES
    vmem = functools.partial(pl.BlockSpec, memory_space=pltpu.VMEM)
    dma = pltpu.SemaphoreType.DMA
    wide = pltpu.VMEM((count, LANES, LANES), F32)
    whole = pltpu.VMEM((peers, cap, LANES), F32)
    half = pltpu.VMEM((peers, cap // 2, LANES), F32)
    solution, resistance = pl.pallas_call(
        functools.partial(kernel, peers, cap),
        out_shape=(jax.ShapeDtypeStruct((width, VERT_DEV), F32), jax.ShapeDtypeStruct((count, LANES), F32)),
        in_specs=[pl.BlockSpec(memory_space=pltpu.SMEM)] + [vmem()] * 5,
        out_specs=(vmem(), vmem()),
        scratch_shapes=[
            pltpu.VMEM((count, 2 * edges, 2 * LANES), BF16),
            pltpu.VMEM((2 * count, LANES, LANES), F32),
            pltpu.VMEM((count, 8, LANES), F32),
            pltpu.VMEM((2 * edges, 2 * LANES), F32),
            whole, wide, wide, wide, wide,
            pltpu.VMEM((2 * count, LANES, LANES), F32),
            pltpu.VMEM((2 * edges, 2 * LANES), BF16),
            pltpu.VMEM((count, LANES), F32),
            pltpu.VMEM((count, LANES), F32),
            pltpu.VMEM((count, LANES), F32),
            pltpu.VMEM((peers, 8, LANES), F32),
            half,
            pltpu.VMEM((peers, 8, LANES), F32),
            half, whole, whole, half, half,
            dma((peers,)), dma((peers,)), dma((peers,)), dma((peers,)), dma((peers,)), dma((peers,)),
            dma, dma,
        ],
        compiler_params=pltpu.CompilerParams(
            collective_id=0, has_side_effects=True, vmem_limit_bytes=60 * 1024 * 1024
        ),
    )(
        send_counts, src_local.reshape(count, LANES), dst_local.reshape(peers, cap),
        edge_weight.reshape(peers, cap), edge_weight.reshape(count, LANES), sketch,
    )
    return solution, resistance.reshape(edges)


def solution(mesh):
    in_specs = (P("dom"), P("dom"), P("dom"), P("dom", None), P("col", "dom"))
    out_specs = (P("col", "dom"), P("dom"))
    return jax.shard_map(local, mesh=mesh, in_specs=in_specs, out_specs=out_specs, check_vma=False)
```

```python
import functools

import jax
import jax.numpy as jnp
from jax import lax
from jax.experimental import pallas as pl
from jax.experimental.pallas import tpu as pltpu
from jax.sharding import PartitionSpec as P

MESH = pl.DeviceIdType.MESH
F32 = jnp.float32
BF16 = jnp.bfloat16
VERT_DEV = 4096
SKETCH = 128
SWEEPS = 3
LANES = 128
HALF = 64
ground_shift = 1.0
degree_boost = 0.25


def either(a, b, n):
    total, bit = 0, 1
    while bit < n:
        total = total + bit * lax.rem(lax.div(a, bit) + lax.div(b, bit), 2)
        bit *= 2
    return total


def kernel(
    peers, cap, counts_ref, src_ref, dst_ref, flat_ref, weight_ref, sketch_ref, sol_ref, res_ref,
    same, ids, rows, acc, field, resid, total, inv, keep, wide, ends, part, part_in,
    live_ref, meta_ref, root_ref, meta_in, root_in, one_in, two_in, last_out, last_in,
    meta_s, meta_r, even_s, even_r, odd_s, odd_r, part_s, part_r,
):
    me = lax.axis_index("dom")
    other = 1 - lax.axis_index("col")
    group = LANES // cap
    count = peers // group
    own_group = lax.div(me, group)

    barrier = pltpu.get_barrier_semaphore()

    def greet(i, _):
        pl.semaphore_signal(barrier, inc=1, device_id={"dom": either(me, i, peers)}, device_id_type=MESH)
        return 0

    lax.fori_loop(1, peers, greet, 0)
    pl.semaphore_signal(barrier, inc=1, device_id={"col": other}, device_id_type=MESH)

    def copy(p, source, target, s, r):
        return pltpu.make_async_remote_copy(
            src_ref=source.at[p], dst_ref=target.at[me], send_sem=s.at[p], recv_sem=r.at[me],
            device_id={"dom": p}, device_id_type=MESH,
        )

    def arrival(p, source, target, s, r):
        return pltpu.make_async_remote_copy(
            src_ref=source.at[p], dst_ref=target.at[p], send_sem=s.at[p], recv_sem=r.at[p],
            device_id={"dom": p}, device_id_type=MESH,
        )

    def send_group(far, source, target, s, r):
        for j in range(group):
            i = far * group + j
            p = either(me, i, peers)

            @pl.when(i != 0)
            def _():
                copy(p, source, target, s, r).start()

            @pl.when(i == 0)
            def _():
                target[me] = source[me]

    def wait_group(far, source, target, s, r):
        for j in range(group):
            i = far * group + j
            p = either(me, i, peers)

            @pl.when(i != 0)
            def _():
                arrival(p, source, target, s, r).wait_recv()

    def wait_sent(source, target, s, r):
        def step(i, _):
            copy(either(me, i, peers), source, target, s, r).wait_send()
            return 0

        lax.fori_loop(1, peers, step, 0)

    low = lax.broadcasted_iota(jnp.int32, (LANES, LANES), 1) < HALF

    def mask(a):
        return low[: a.shape[0]]

    def turned(a):
        return pltpu.roll(a, HALF, axis=1)

    def doubled(a):
        b = turned(a)
        return jnp.where(mask(a), a, b), jnp.where(mask(a), b, a)

    def split(a):
        high = a.astype(BF16).astype(F32)
        return jnp.where(low, high, a - high).astype(BF16)

    def column(row):
        return jnp.broadcast_to(row, (LANES, LANES)).T

    def short(a):
        return a.astype(jnp.int32).astype(jnp.int16)

    def equal(name, row):
        row = short(jnp.broadcast_to(row, (LANES, LANES)))
        return jnp.where(name == row[None], jnp.array(1, BF16), jnp.array(0, BF16)).reshape(-1, LANES)

    def unfold(ref, g):
        pieces = []
        for j in range(group):
            pieces.extend(doubled(ref[g * group + j]))
        return jnp.concatenate(pieces, axis=0)

    def block(ref, g):
        return ref[pl.ds(g * group, group)].reshape(LANES, LANES)

    def near_first(t):
        return either(own_group, lax.rem(count - t, count), count), lax.rem(count - t, count)

    spot = lax.broadcasted_iota(jnp.int32, (1, LANES), 1)

    def message(p, _):
        alive = jnp.where(spot[:, :cap] < counts_ref[0, p], 1.0, 0.0)
        meta_ref[p, 0:1, 0:cap] = dst_ref[pl.ds(p, 1), :].astype(F32)
        meta_ref[p, 1:2, 0:cap] = flat_ref[pl.ds(p, 1), :] * alive
        return 0

    meta_ref[...] = jnp.zeros_like(meta_ref)
    lax.fori_loop(0, peers, message, 0, unroll=4)
    pl.semaphore_wait(barrier, peers)

    def send_meta(t, _):
        send_group(count - 1 - t, meta_ref, meta_in, meta_s, meta_r)
        return 0

    lax.fori_loop(0, count, send_meta, 0)

    def send_root(t, _):
        far = count - 1 - t
        g = either(own_group, far, count)
        alive = jnp.zeros((1, LANES), F32)
        for j in range(group):
            there = (spot >= j * cap) & (spot < j * cap + counts_ref[0, g * group + j])
            alive = jnp.where(there, 1.0, alive)
        live_ref[pl.ds(g, 1), :] = alive
        heavy = weight_ref[pl.ds(g, 1), :] * alive
        wide[g] = column(heavy)
        at = pl.ds(pl.multiple_of(g * LANES, LANES), LANES)
        value = jnp.sqrt(heavy) * sketch_ref[:, at].astype(F32)
        value = jnp.concatenate([value, value], axis=0).T
        total[g] = value
        for j in range(group):
            a = value[j * cap : j * cap + cap // 2]
            b = value[j * cap + cap // 2 : (j + 1) * cap]
            root_ref[g * group + j] = jnp.where(mask(a), a, b)
        send_group(far, root_ref, root_in, even_s, even_r)
        return 0

    lax.fori_loop(0, count, send_root, 0)

    def first_ends(g, _):
        row = src_ref[pl.ds(g, 1), :].astype(F32)
        rows[g, 0:1] = row
        ids[g] = short(column(row))
        return 0

    lax.fori_loop(0, count, first_ends, 0, unroll=4)

    def take_meta(t, _):
        wait_group(t, meta_ref, meta_in, meta_s, meta_r)
        return 0

    lax.fori_loop(0, count, take_meta, 0)

    def second_ends(g, _):
        named = [column(meta_in[g * group + j][0:1])[:cap] for j in range(group)]
        named = jnp.concatenate(named, axis=0)
        heavy = [column(meta_in[g * group + j][1:2])[:cap] for j in range(group)]
        heavy = jnp.concatenate(heavy, axis=0)
        ids[count + g] = short(named)
        rows[g, 1:2] = named.T[0:1]
        wide[count + g] = heavy
        return 0

    lax.fori_loop(0, count, second_ends, 0, unroll=4)

    tile = 512
    blocks = tile // LANES
    tiles = 2 * count // blocks

    acc[...] = jnp.zeros_like(acc)

    def first_product(t, _):
        g, far = near_first(t)
        wait_group(far, root_ref, root_in, even_s, even_r)
        value = jnp.concatenate([split(total[g]), split(-unfold(root_in, g))], axis=0)
        load = jnp.concatenate([split(wide[g]), split(wide[count + g])], axis=0)
        x = jnp.concatenate([value, load], axis=1)
        row_u, row_v = rows[g, 0:1], rows[g, 1:2]

        for k in range(tiles):
            at = pl.ds(k * tile, tile)
            name = ids[pl.ds(k * blocks, blocks)]
            e = jnp.concatenate([equal(name, row_u), equal(name, row_v)], axis=1)
            same[g, at, :] = e
            acc[at, :] += jnp.dot(e, x, preferred_element_type=F32)
        return 0

    lax.fori_loop(0, count, first_product, 0)
    wait_sent(meta_ref, meta_in, meta_s, meta_r)
    wait_sent(root_ref, root_in, even_s, even_r)

    def at_ends(g, lane):
        a = acc[pl.ds(pl.multiple_of(g * LANES, LANES), LANES), lane : lane + LANES]
        b = acc[pl.ds(pl.multiple_of((count + g) * LANES, LANES), LANES), lane : lane + LANES]
        return jnp.where(low, a + turned(a), b + turned(b))

    def put(ref, g, value):
        ref[pl.ds(g * group, group)] = value.reshape(group, cap, LANES)

    def start_field(t, _):
        far = count - 1 - t
        g = either(own_group, far, count)
        degree = at_ends(g, LANES)
        one_over = 1.0 / ((1.0 + degree_boost) * degree + ground_shift)
        inv[g] = one_over
        keep[g] = (degree_boost * degree + ground_shift) * one_over
        d = at_ends(g, 0) * one_over
        put(field, g, d)
        send_group(far, field, one_in, odd_s, odd_r)
        resid[g] = d
        total[g] = d
        wide[g] = jnp.where(low, wide[g], wide[count + g])
        return 0

    lax.fori_loop(0, count, start_field, 0)

    def multiply(came, s, r):
        acc[:, 0:LANES] = jnp.zeros((2 * count * LANES, LANES), F32)

        def product(t, _):
            g, far = near_first(t)
            wait_group(far, field, came, s, r)
            flow = wide[g] * (block(field, g) - turned(block(came, g)))
            flow_u, flow_v = doubled(flow)
            x = jnp.concatenate([split(flow_u), split(flow_v)], axis=0)

            for k in range(tiles):
                at = pl.ds(k * tile, tile)
                acc[at, 0:LANES] += jnp.dot(same[g, at, :], x, preferred_element_type=F32)
            return 0

        lax.fori_loop(0, count, product, 0)
        wait_sent(field, came, s, r)

    sigma, delta = 1.25, 0.8
    coeff = 1.0 / sigma
    newer = 1.0 / (2.0 * sigma - coeff)
    pairs = ((newer * coeff, 2.0 * newer / delta),)
    coeff = newer
    newer = 1.0 / (2.0 * sigma - coeff)
    pairs += ((newer * coeff, 2.0 * newer / delta),)

    multiply(one_in, odd_s, odd_r)

    def second_field(t, _):
        far = count - 1 - t
        g = either(own_group, far, count)
        d = block(field, g)
        r = resid[g] - (at_ends(g, 0) * inv[g] + keep[g] * d)
        d = pairs[0][0] * d + pairs[0][1] * r
        put(field, g, d)
        send_group(far, field, two_in, even_s, even_r)
        resid[g] = r
        total[g] = total[g] + d
        return 0

    lax.fori_loop(0, count, second_field, 0)
    multiply(two_in, even_s, even_r)

    def third_field(t, _):
        far = count - 1 - t
        g = either(own_group, far, count)
        d = block(field, g)
        r = resid[g] - (at_ends(g, 0) * inv[g] + keep[g] * d)
        d = pairs[1][0] * d + pairs[1][1] * r
        whole = total[g] + d
        total[g] = whole
        for j in range(group):
            a = whole[j * cap : j * cap + cap // 2]
            b = whole[j * cap + cap // 2 : (j + 1) * cap]
            last_out[g * group + j] = jnp.where(mask(a), turned(a), b)
        send_group(far, last_out, last_in, odd_s, odd_r)
        whole_u, whole_v = doubled(whole)
        ones = jnp.ones((2 * LANES, LANES), BF16)
        pair = jnp.concatenate([split(whole_u), split(whole_v)], axis=0)
        at = pl.ds(pl.multiple_of(g * 2 * LANES, 2 * LANES), 2 * LANES)
        ends[at, :] = jnp.concatenate([pair, ones], axis=1)
        return 0

    lax.fori_loop(0, count, third_field, 0)

    strip = 256

    def vertices(k, _):
        first = k * strip
        name = (lax.broadcasted_iota(jnp.int32, (strip, LANES), 0) + first).astype(F32)
        e = [
            jnp.where(name == rows[g, j : j + 1], 1.0, 0.0).astype(BF16) for g in range(count) for j in range(2)
        ]
        out = jnp.dot(jnp.concatenate(e, axis=1), ends[...], preferred_element_type=F32)
        value = out[:, 0:LANES]
        value = (value + turned(value)) / jnp.maximum(out[:, LANES:], 1.0)
        sol_ref[:, pl.ds(pl.multiple_of(first, strip), strip)] = value.T[0:HALF]
        return 0

    lax.fori_loop(0, VERT_DEV // strip, vertices, 0)

    def differences(t, _):
        g, far = near_first(t)
        wait_group(far, last_out, last_in, odd_s, odd_r)
        diff = jnp.where(low, total[g] - unfold(last_in, g), 0.0)
        part[pl.ds(g, 1), :] = jnp.sum((diff * diff).T, axis=0, keepdims=True)
        return 0

    lax.fori_loop(0, count, differences, 0)
    wait_sent(last_out, last_in, odd_s, odd_r)

    swap = pltpu.make_async_remote_copy(
        src_ref=part, dst_ref=part_in, send_sem=part_s, recv_sem=part_r,
        device_id={"col": other}, device_id_type=MESH,
    )
    swap.start()
    swap.wait()
    res_ref[...] = (part[...] + part_in[...]) / SKETCH * live_ref[...]


def local(src_local, dst_local, edge_weight, send_counts, sketch):
    peers = lax.axis_size("dom")
    edges = src_local.shape[0]
    cap = edges // peers
    width = sketch.shape[0]
    count = edges // LANES
    vmem = functools.partial(pl.BlockSpec, memory_space=pltpu.VMEM)
    dma = pltpu.SemaphoreType.DMA
    wide = pltpu.VMEM((count, LANES, LANES), F32)
    whole = pltpu.VMEM((peers, cap, LANES), F32)
    half = pltpu.VMEM((peers, cap // 2, LANES), F32)
    solution, resistance = pl.pallas_call(
        functools.partial(kernel, peers, cap),
        out_shape=(jax.ShapeDtypeStruct((width, VERT_DEV), F32), jax.ShapeDtypeStruct((count, LANES), F32)),
        in_specs=[pl.BlockSpec(memory_space=pltpu.SMEM)] + [vmem()] * 5,
        out_specs=(vmem(), vmem()),
        scratch_shapes=[
            pltpu.VMEM((count, 2 * edges, 2 * LANES), BF16),
            pltpu.VMEM((2 * count, LANES, LANES), jnp.int16),
            pltpu.VMEM((count, 8, LANES), F32),
            pltpu.VMEM((2 * edges, 2 * LANES), F32),
            whole, wide, wide, wide, wide,
            pltpu.VMEM((2 * count, LANES, LANES), F32),
            pltpu.VMEM((2 * edges, 2 * LANES), BF16),
            pltpu.VMEM((count, LANES), F32),
            pltpu.VMEM((count, LANES), F32),
            pltpu.VMEM((count, LANES), F32),
            pltpu.VMEM((peers, 8, LANES), F32),
            half,
            pltpu.VMEM((peers, 8, LANES), F32),
            half, whole, whole, half, half,
            dma((peers,)), dma((peers,)), dma((peers,)), dma((peers,)), dma((peers,)), dma((peers,)),
            dma, dma,
        ],
        compiler_params=pltpu.CompilerParams(
            collective_id=0, has_side_effects=True, vmem_limit_bytes=60 * 1024 * 1024
        ),
    )(
        send_counts, src_local.reshape(count, LANES), dst_local.reshape(peers, cap),
        edge_weight.reshape(peers, cap), edge_weight.reshape(count, LANES), sketch,
    )
    return solution, resistance.reshape(edges)


def solution(mesh):
    in_specs = (P("dom"), P("dom"), P("dom"), P("dom", None), P("col", "dom"))
    out_specs = (P("col", "dom"), P("dom"))
    return jax.shard_map(local, mesh=mesh, in_specs=in_specs, out_specs=out_specs, check_vma=False)
```
